256 devices in a mesh: row: 32 (over y, x, z_lo), col: 8 (over z_hi, core).
Axes of the slice: x: 4, y: 4, z: 8 (z_hi: 4, z_lo: 2; z = z_hi * 2 + z_lo), core: 2. Of those that a mesh axis runs over, the one named last changes fastest.
Arguments:
- feature_codes: int32 [131072, 256], P(('row', 'col')), may hold values from -127 to 127
- bit_widths: int32 [256], P(('row', 'col')), may hold values from 4 to 8
- row_scales: float32 [131072], P(('row', 'col')), may hold values from 0.003 to 0.03
- weight: bfloat16 [256, 256], P('col'), may hold values from -0.375 to 0.375
- layer_bias: float32 [256], replicated, may hold values from -3 to 3
- adjacency_blocks: bfloat16 [1024, 8, 11, 128, 128], P('row', 'col'), may hold values from 0.0049743652 to 0.099609375
- block_index: int32 [1024, 8, 11], P('row', 'col'), may hold values from 0 to 127
- block_counts: int32 [1024, 8], P('row', 'col'), may hold values from 1 to 11, as said below
Outputs:
- aggregated: bfloat16 [131072, 256], P(('row', 'col'))
The draws below stay inside these ranges and needn't reach their ends.
Inputs may be any that keep to these rules, and one draw needn't show every extreme that they name: `block_index`: column blocks within a column group. `block_counts`: row blocks of one device may differ in live slots; some row block uses all 11.
All inputs are finite; a program needn't handle non-finite values.
Results may differ from the reference program's by a relative error of at most 0.0041.
Values may be sent and summed in bfloat16 or wider, within the bound.
No kernel may reach another device: no remote copies, remote signals or barrier semaphores. Data moves between devices by JAX's collectives and lax.ppermute only.
A program may use at most 128 MiB of HBM per device.

```python
import math
import jax
import jax.numpy as jnp
import numpy as np
from jax import lax

F = 256
BLOCK = 128
MAXB = 11
SUB = 512
NODES = 131072
RB = 32
NCB = 128
N_ROW = 32
N_COL = 8


def draw_block_counts(key, part):
    key = jax.random.fold_in(key, 11)
    key_level, key_pick, key_raw, key_where = jax.random.split(key, 4)
    level = jax.random.randint(key_level, (N_ROW, 1, N_COL), 2, MAXB + 1)
    chosen = jax.random.randint(key_pick, (), 0, N_ROW * N_COL)
    device_id = jnp.arange(N_ROW)[:, None, None] * N_COL + jnp.arange(N_COL)[None, None, :]
    level = jnp.where(device_id == chosen, MAXB, level)
    raw_counts = jax.random.randint(key_raw, (N_ROW, RB, N_COL), 1, MAXB + 1)
    counts = jnp.minimum(raw_counts, level)
    position = jax.random.randint(key_where, (N_ROW, 1, N_COL), 0, RB)
    counts = jnp.where(jnp.arange(RB)[None, :, None] == position, level, counts)
    return counts.reshape(N_ROW * RB, N_COL).astype(jnp.int32)


def plant(array, stream_key, smallest, high):
    extent = array.shape
    place = [jax.random.randint(jax.random.fold_in(stream_key, axis), (), 0, extent[axis]) for axis in range(len(extent))]
    array = array.at[tuple(place)].set(smallest)
    longest = extent.index(max(extent))
    place[longest] = (place[longest] + 1) % extent[longest]
    return array.at[tuple(place)].set(high)


def block_levels(own_key, extent, cuts, least, largest):
    factor_of, own = 1.0, jax.random.fold_in(own_key, 6)
    for dim, parts in cuts:
        steps = jnp.exp(jax.random.uniform(jax.random.fold_in(own, dim), (parts,), jnp.float32, least / len(cuts), largest / len(cuts)))
        factor_of = factor_of * jnp.repeat(steps, extent[dim] // parts).reshape([-1 if axis == dim else 1 for axis in range(len(extent))])
    return factor_of


def cumulative_ranks(amount, skew):
    portions = [(1 << 20) // math.isqrt(standing ** skew) + 1 for standing in range(1, amount + 1)]
    width = 1 + sum(portions) // (1 << 30)
    return np.cumsum(np.array([max(1, weight // width) for weight in portions]))


def skewed_ids(key, dims, number_of, skew):
    grid = cumulative_ranks(number_of, skew)
    ticket = jax.random.randint(jax.random.fold_in(key, 1), dims, 0, int(grid[number_of - 1]))
    standing = jnp.searchsorted(jnp.asarray(grid, jnp.int32), ticket, side="right")
    return jax.random.permutation(jax.random.fold_in(key, 2), number_of)[standing].astype(jnp.int32)


def bell_draw(own_key, dims, width, limit, cuts=(), kind=jnp.bfloat16):
    array = width * jax.random.normal(own_key, dims, jnp.float32)
    if cuts:
        array = array * block_levels(own_key, dims, cuts, -0.22, 0.18)
    return jnp.clip(array, -limit, limit).astype(kind)


def setup_inputs(seed: int = 0) -> dict:
    keys = jax.random.split(jax.random.key(seed), 9)
    feature_codes = plant(jax.random.randint(keys[0], (NODES, F), -127, 128), jax.random.fold_in(keys[0], 1), -127, 127).astype(jnp.int32)
    bit_widths = plant(jax.random.randint(keys[1], (N_ROW * N_COL,), 4, 9), jax.random.fold_in(keys[1], 1), 4, 8).astype(jnp.int32)
    row_scales = jnp.clip(jnp.exp(math.log(0.03) - 2.3025851 * jax.random.uniform(keys[2], (NODES,), jnp.float32) ** block_levels(keys[2], (NODES,), ((0, 256),), -0.2, 0.2)), 0.003, 0.03)
    weight = bell_draw(keys[3], (F, F), F ** -0.5, 0.375, ((0, 8),))
    layer_bias = bell_draw(keys[4], (F,), 0.5, 3.0, (), jnp.float32)
    adjacency_blocks = jnp.clip(jnp.exp(math.log(0.099609375) - 2.9969585 * jax.random.uniform(keys[5], (N_ROW * RB, N_COL, MAXB, BLOCK, BLOCK), jnp.float32) ** block_levels(keys[5], (N_ROW * RB, N_COL, MAXB, BLOCK, BLOCK), ((0, 32), (1, 8)), -0.2, 0.2)), 0.0049743652, 0.099609375).astype(jnp.bfloat16)
    block_index = plant(skewed_ids(keys[6], (N_ROW * RB, N_COL, MAXB), NCB, 2), jax.random.fold_in(keys[6], 3), 0, NCB - 1).astype(jnp.int32)
    block_counts = draw_block_counts(jax.random.fold_in(keys[8], 71), 0)
    return dict(feature_codes=feature_codes, bit_widths=bit_widths, row_scales=row_scales, weight=weight, layer_bias=layer_bias, adjacency_blocks=adjacency_blocks, block_index=block_index, block_counts=block_counts)


def reference(feature_codes, bit_widths, row_scales, weight, layer_bias, adjacency_blocks, block_index, block_counts):
    unit = jnp.left_shift(jnp.ones_like(bit_widths), 8 - bit_widths)
    unit_rows = jnp.repeat(unit, SUB)[:, None]
    level = jnp.floor_divide(feature_codes, unit_rows) * unit_rows
    features = (level.astype(jnp.float32) * row_scales[:, None]).astype(jnp.bfloat16)
    hidden = jnp.dot(features, weight, preferred_element_type=jnp.float32).astype(jnp.bfloat16)
    panels = hidden.reshape(N_ROW, N_COL, SUB, F)
    blocks_parts = adjacency_blocks.reshape(N_ROW, RB, N_COL, MAXB, BLOCK, BLOCK)
    index_parts = block_index.reshape(N_ROW, RB, N_COL, MAXB)
    count_parts = block_counts.reshape(N_ROW, RB, N_COL)
    slots = jnp.arange(MAXB, dtype=jnp.int32)

    def one_partition(items):
        part_blocks, part_index, part_counts = items
        running = jnp.zeros((RB, BLOCK, F), jnp.float32)
        for col_part in range(N_COL):
            columns = panels[:, col_part].reshape(NCB, BLOCK, F)
            picked = columns[part_index[:, col_part]]
            live_mask = slots[None, :] < part_counts[:, col_part][:, None]
            picked = jnp.where(live_mask[:, :, None, None], picked, jnp.zeros_like(picked))
            running = running + jnp.einsum("rmij,rmjf->rif", part_blocks[:, col_part].astype(jnp.float32), picked.astype(jnp.float32))
        return running.reshape(RB * BLOCK, F)

    summed = lax.map(one_partition, (blocks_parts, index_parts, count_parts)).reshape(NODES, F)
    return jnp.maximum(summed + layer_bias[None, :], 0.0).astype(jnp.bfloat16)
```

```python
import functools

import jax
import jax.numpy as jnp
from jax import lax
from jax.experimental import pallas as pl
from jax.experimental.pallas import tpu as pltpu
from jax.sharding import PartitionSpec as P

NX, NY, NZ = 4, 4, 2
NH = 4
PANEL = 512
BLOCK = 128
F = 256
RB = 32
MAXB = 11
KPER = PANEL // BLOCK

PLAN = (
    (0, -1, (0, 0, 0)),
    (0, 1, (0, 0, 0)),
    (1, -1, (0, 0, 0)),
    (1, 1, (0, 0, 0)),
    (2, 1, (0, 0, 0)),
    (0, -1, (0, 1, 0)),
    (0, 1, (0, 3, 0)),
    (1, -1, (3, 0, 0)),
    (1, 1, (0, 0, 1)),
    (2, 1, (1, 0, 0)),
    (0, 1, (1, 0, 0)),
    (1, -1, (0, 0, 1)),
    (1, 1, (0, 1, 0)),
    (2, 1, (3, 0, 0)),
    (0, -1, (0, 1, 1)),
    (0, 1, (0, 1, 0)),
    (1, -1, (3, 3, 0)),
    (1, 1, (0, 1, 1)),
    (2, 1, (1, 3, 0)),
    (0, -1, (3, 1, 0)),
    (0, 1, (0, 2, 0)),
    (1, -1, (2, 0, 0)),
    (1, 1, (1, 0, 1)),
    (2, 1, (2, 0, 0)),
    (0, -1, (3, 1, 1)),
    (0, 1, (1, 3, 1)),
    (1, -1, (1, 3, 1)),
    (1, 1, (2, 1, 0)),
    (2, 1, (3, 3, 0)),
    (0, -1, (0, 2, 1)),
    (1, 1, (2, 1, 1)),
)


def row_perm(axis, step):
    pairs = []
    for y in range(NY):
        for x in range(NX):
            for z in range(NZ):
                c = [x, y, z]
                c[axis] = (c[axis] + step) % (NX, NY, NZ)[axis]
                pairs.append(((y * NX + x) * NZ + z, (c[1] * NX + c[0]) * NZ + c[2]))
    return pairs


def col_perm(dz, core):
    return [(h * 2 + c, ((h + dz) % NH) * 2 + (c ^ core)) for h in range(NH) for c in range(2)]


def gather_rows(mine):
    held = {(0, 0, 0): mine}
    for axis, step, source in PLAN:
        target = list(source)
        target[axis] = (target[axis] + step) % (NX, NY, NZ)[axis]
        held[tuple(target)] = lax.ppermute(held[source], "row", row_perm(axis, step))
    return [held[(a, b, c)] for a in range(NX) for b in range(NY) for c in range(NZ)]


def gather_weight(weight):
    swapped = lax.ppermute(weight, "col", col_perm(0, 1))
    core = lax.rem(lax.axis_index("col"), 2)
    pair = jnp.where(core == 0, jnp.concatenate([weight, swapped]), jnp.concatenate([swapped, weight]))
    parts = [pair] + [lax.ppermute(pair, "col", col_perm(d, 0)) for d in (1, 2, 3)]
    chip = lax.div(lax.axis_index("col"), 2)
    stacked = jnp.stack(parts)
    order = jnp.remainder(chip - jnp.arange(NH), NH)
    return stacked[order].reshape(F, F)


def aggregate_kernel(order_ref, index_ref, count_ref, adj_ref, weight_ref, *refs):
    pieces = refs[: NX * NY * NZ]
    send_ref, keep_ref, hidden, sems = refs[NX * NY * NZ :]
    i = pl.program_id(0)

    @pl.when(i == 0)
    def _():
        copies = [
            pltpu.make_async_copy(piece, hidden.at[pl.ds(n * PANEL, PANEL)], sems.at[n])
            for n, piece in enumerate(pieces)
        ]
        for copy in copies:
            copy.start()
        for n, copy in enumerate(copies):
            copy.wait()
            rows = pl.ds(n * PANEL, PANEL)
            hidden[rows, :] = jnp.dot(
                hidden[rows, :], weight_ref[...], preferred_element_type=jnp.float32
            ).astype(jnp.bfloat16)

    block = order_ref[i]
    count = count_ref[block]

    def rows_of(slot):
        start = pl.multiple_of(index_ref[block * MAXB + slot] * BLOCK, BLOCK)
        return hidden[pl.ds(start, BLOCK), :]

    def pair(p, total):
        first = 2 * p
        second = jnp.minimum(first + 1, MAXB - 1)
        live = (first + 1 < count).astype(jnp.float32).astype(jnp.bfloat16)
        left = jnp.concatenate([adj_ref[0, 0, first], adj_ref[0, 0, second] * live], axis=1)
        right = jnp.concatenate([rows_of(first), rows_of(second)], axis=0)
        return total + jnp.dot(left, right, preferred_element_type=jnp.float32)

    total = lax.fori_loop(0, lax.div(count + 1, 2), pair, jnp.zeros((BLOCK, F), jnp.float32))

    @pl.when(i < RB // 2)
    def _():
        send_ref[...] = total.astype(jnp.bfloat16)

    @pl.when(i >= RB // 2)
    def _():
        keep_ref[...] = total


def aggregate(order, index, counts, adjacency, weight, pieces):
    half = RB // 2
    return pl.pallas_call(
        aggregate_kernel,
        grid_spec=pltpu.PrefetchScalarGridSpec(
            num_scalar_prefetch=3,
            grid=(RB,),
            in_specs=[
                pl.BlockSpec((1, 1, MAXB, BLOCK, BLOCK), lambda i, order, index, counts: (order[i], 0, 0, 0, 0)),
                pl.BlockSpec((F, F), lambda i, order, index, counts: (0, 0)),
            ]
            + [pl.BlockSpec(memory_space=pl.ANY)] * len(pieces),
            out_specs=[
                pl.BlockSpec((BLOCK, F), lambda i, order, index, counts: (jnp.minimum(i, half - 1), 0)),
                pl.BlockSpec((BLOCK, F), lambda i, order, index, counts: (jnp.maximum(i - half, 0), 0)),
            ],
            scratch_shapes=[
                pltpu.VMEM((NX * NY * NZ * PANEL, F), jnp.bfloat16),
                pltpu.SemaphoreType.DMA((NX * NY * NZ,)),
            ],
        ),
        out_shape=[
            jax.ShapeDtypeStruct((half * BLOCK, F), jnp.bfloat16),
            jax.ShapeDtypeStruct((half * BLOCK, F), jnp.float32),
        ],
        compiler_params=pltpu.CompilerParams(vmem_limit_bytes=24 << 20),
    )(order, index, counts, adjacency, weight, *pieces)


def reduce_chips(send, keep):
    got = lax.ppermute(send, "col", col_perm(0, 1))
    h = PANEL // 2

    def part(d, side):
        at = d * PANEL + side * h
        return keep[at : at + h] + got[at : at + h].astype(jnp.float32)

    def plus(value):
        return lax.ppermute(value.astype(jnp.bfloat16), "col", col_perm(1, 0)).astype(jnp.float32)

    def minus(value):
        return lax.ppermute(value.astype(jnp.bfloat16), "col", col_perm(-1, 0)).astype(jnp.float32)

    far_top = plus(part(2, 0))
    far_bottom = minus(part(2, 1))
    near_bottom = plus(part(1, 1))
    near_top = minus(part(3, 0))
    chain_top = plus(part(1, 0) + far_top)
    chain_bottom = minus(part(3, 1) + far_bottom)
    top = part(0, 0) + near_top + chain_top
    bottom = part(0, 1) + near_bottom + chain_bottom
    return jnp.concatenate([top, bottom])


def on_device(
    feature_codes,
    bit_widths,
    row_scales,
    weight,
    layer_bias,
    adjacency_blocks,
    block_index,
    block_counts,
):
    row, col = lax.axis_index("row"), lax.axis_index("col")
    shift = 8 - bit_widths[0]
    level = jnp.left_shift(jnp.right_shift(feature_codes, shift), shift)
    features = (level.astype(jnp.float32) * row_scales[:, None]).astype(jnp.bfloat16)
    pieces = gather_rows(features)
    full_weight = gather_weight(weight)

    y, x, z = row // (NX * NZ), (row // NZ) % NX, row % NZ
    source, k = block_index[:, 0] // KPER, block_index[:, 0] % KPER
    dx = jnp.remainder(x - (source // NZ) % NX, NX)
    dy = jnp.remainder(y - source // (NX * NZ), NY)
    dz = jnp.remainder(z - source % NZ, NZ)
    index = (((dx * NY + dy) * NZ + dz) * KPER + k).reshape(RB * MAXB)

    chip, core = col // 2, col % 2
    step = jnp.arange(RB)
    d, other = (step // KPER) % NH, jnp.where(step < RB // 2, 1 - core, core)
    order = (jnp.remainder(chip + d, NH) * 2 + other) * KPER + step % KPER
    send, keep = aggregate(
        order.astype(jnp.int32), index, block_counts[:, 0], adjacency_blocks, full_weight, pieces
    )
    summed = reduce_chips(send, keep)
    return jnp.maximum(summed + layer_bias[None, :], 0.0).astype(jnp.bfloat16)


def solution(mesh):
    in_specs = (
        P(("row", "col"), None),
        P(("row", "col")),
        P(("row", "col")),
        P("col", None),
        P(),
        P("row", "col", None, None, None),
        P("row", "col", None),
        P("row", "col"),
    )
    out_specs = P(("row", "col"), None)
    return jax.shard_map(
        on_device, mesh=mesh, in_specs=in_specs, out_specs=out_specs, check_vma=False
    )
```

```python
import jax
import jax.numpy as jnp
from jax import lax
from jax.experimental import pallas as pl
from jax.experimental.pallas import tpu as pltpu
from jax.sharding import PartitionSpec as P

NX, NY, NZ = 4, 4, 2
NH = 4
PANEL = 512
BLOCK = 128
F = 256
RB = 32
MAXB = 11
KPER = PANEL // BLOCK
SHARDS = NX * NY * NZ
ADJ_COPIES = 4
TILE = 8
GROUP = 4

PLAN = (
    (0, -1, (0, 0, 0)),
    (0, 1, (0, 0, 0)),
    (1, -1, (0, 0, 0)),
    (1, 1, (0, 0, 0)),
    (2, 1, (0, 0, 0)),
    (0, -1, (0, 1, 0)),
    (0, 1, (0, 3, 0)),
    (1, -1, (3, 0, 0)),
    (1, 1, (0, 0, 1)),
    (2, 1, (1, 0, 0)),
    (0, 1, (1, 0, 0)),
    (1, -1, (0, 0, 1)),
    (1, 1, (0, 1, 0)),
    (2, 1, (3, 0, 0)),
    (0, -1, (0, 1, 1)),
    (0, 1, (0, 1, 0)),
    (1, -1, (3, 3, 0)),
    (1, 1, (0, 1, 1)),
    (2, 1, (1, 3, 0)),
    (0, -1, (3, 1, 0)),
    (0, 1, (0, 2, 0)),
    (1, -1, (2, 0, 0)),
    (1, 1, (1, 0, 1)),
    (2, 1, (2, 0, 0)),
    (0, -1, (3, 1, 1)),
    (0, 1, (1, 3, 1)),
    (1, -1, (1, 3, 1)),
    (1, 1, (2, 1, 0)),
    (2, 1, (3, 3, 0)),
    (0, -1, (0, 2, 1)),
    (1, 1, (2, 1, 1)),
)


def row_perm(axis, step):
    pairs = []
    for y in range(NY):
        for x in range(NX):
            for z in range(NZ):
                c = [x, y, z]
                c[axis] = (c[axis] + step) % (NX, NY, NZ)[axis]
                pairs.append(((y * NX + x) * NZ + z, (c[1] * NX + c[0]) * NZ + c[2]))
    return pairs


def col_perm(dz, core):
    return [(h * 2 + c, ((h + dz) % NH) * 2 + (c ^ core)) for h in range(NH) for c in range(2)]


def after(value, *others):
    return lax.optimization_barrier((value, *others))[0]


def gather_rows(mine):
    held, last = {(0, 0, 0): mine}, {}
    for axis, step, source in PLAN:
        target = list(source)
        target[axis] = (target[axis] + step) % (NX, NY, NZ)[axis]
        value, link = held[source], (axis, step)
        if link in last:
            value = after(value, last[link])
        last[link] = held[tuple(target)] = lax.ppermute(value, "row", row_perm(axis, step))
    return [held[(a, b, c)] for a in range(NX) for b in range(NY) for c in range(NZ)]


def gather_weight(weight):
    pair = jnp.concatenate([weight, lax.ppermute(weight, "col", col_perm(0, 1))])
    quad = jnp.concatenate([pair, lax.ppermute(pair, "col", col_perm(1, 0))])
    whole = jnp.concatenate([quad, lax.ppermute(quad, "col", col_perm(2, 0))])
    return whole.reshape(NH * 2, F // (NH * 2), F)


def aggregate_kernel(order_ref, index_ref, place_ref, weight_ref, adj_hbm, *refs):
    pieces = refs[:SHARDS]
    send_ref, keep_ref, hidden, adj, weight, adj_sems, sems = refs[SHARDS:]
    copies = [
        pltpu.make_async_copy(piece, hidden.at[pl.ds(n * PANEL, PANEL)], sems.at[n])
        for n, piece in enumerate(pieces)
    ]
    part = RB // ADJ_COPIES
    adj_copies = [
        pltpu.make_async_copy(adj_hbm.at[pl.ds(n * part, part), 0], adj.at[pl.ds(n * part, part)], adj_sems.at[n])
        for n in range(ADJ_COPIES)
    ]
    for copy in copies:
        copy.start()
    for copy in adj_copies:
        copy.start()

    rows = F // (NH * 2)
    for n in range(NH * 2):
        weight[pl.ds(pl.multiple_of(place_ref[n] * rows, rows), rows), :] = weight_ref[n]
    hidden[pl.ds(SHARDS * PANEL, BLOCK), :] = jnp.zeros((BLOCK, F), jnp.bfloat16)
    for t in range(0, SHARDS, TILE):
        for copy in copies[t : t + TILE]:
            copy.wait()
        at = pl.ds(t * PANEL, TILE * PANEL)
        hidden[at, :] = jnp.dot(
            hidden[at, :], weight[...], preferred_element_type=jnp.float32
        ).astype(jnp.bfloat16)
    for copy in adj_copies:
        copy.wait()

    def total_of(i):
        block = order_ref[i]
        right = [
            hidden[pl.ds(pl.multiple_of(index_ref[block * MAXB + m] * BLOCK, BLOCK), BLOCK), :]
            for m in range(MAXB)
        ]
        left = [adj[block, m] for m in range(MAXB)]
        return jnp.dot(
            jnp.concatenate(left, axis=1), jnp.concatenate(right, axis=0), preferred_element_type=jnp.float32
        )

    half = RB // 2

    def some(first, out_ref):
        def body(g, _):
            for j in range(GROUP):
                i = g * GROUP + j
                out_ref[pl.ds(pl.multiple_of(i * BLOCK, BLOCK), BLOCK), :] = total_of(first + i).astype(out_ref.dtype)
            return 0

        lax.fori_loop(0, half // GROUP, body, 0)

    some(0, send_ref)
    some(half, keep_ref)


def aggregate(order, index, place, weight_rows, adjacency, pieces):
    half = RB // 2
    smem, vmem, anywhere = (pl.BlockSpec(memory_space=m) for m in (pltpu.SMEM, pltpu.VMEM, pl.ANY))
    return pl.pallas_call(
        aggregate_kernel,
        in_specs=[smem, smem, smem, vmem, anywhere] + [anywhere] * SHARDS,
        out_specs=[vmem, vmem],
        scratch_shapes=[
            pltpu.VMEM((SHARDS * PANEL + BLOCK, F), jnp.bfloat16),
            pltpu.VMEM((RB, MAXB, BLOCK, BLOCK), jnp.bfloat16),
            pltpu.VMEM((F, F), jnp.bfloat16),
            pltpu.SemaphoreType.DMA((ADJ_COPIES,)),
            pltpu.SemaphoreType.DMA((SHARDS,)),
        ],
        out_shape=[
            jax.ShapeDtypeStruct((half * BLOCK, F), jnp.bfloat16),
            jax.ShapeDtypeStruct((half * BLOCK, F), jnp.float32),
        ],
        compiler_params=pltpu.CompilerParams(vmem_limit_bytes=60 << 20),
    )(order, index, place, weight_rows, adjacency, *pieces)


def reduce_chips(send, keep):
    got = lax.ppermute(send, "col", col_perm(0, 1))
    h = PANEL // 2

    def part(d, side):
        at = d * PANEL + side * h
        return keep[at : at + h] + got[at : at + h].astype(jnp.float32)

    def plus(value):
        return lax.ppermute(value.astype(jnp.bfloat16), "col", col_perm(1, 0)).astype(jnp.float32)

    def minus(value):
        return lax.ppermute(value.astype(jnp.bfloat16), "col", col_perm(-1, 0)).astype(jnp.float32)

    first = [part(2, 0), part(2, 1), part(1, 1), part(3, 0)]
    first = lax.optimization_barrier([value.astype(jnp.bfloat16) for value in first])
    far_top, far_bottom = plus(first[0]), minus(first[1])
    near_bottom, near_top = plus(first[2]), minus(first[3])
    chain_top = plus(part(1, 0) + far_top)
    chain_bottom = minus(part(3, 1) + far_bottom)
    top = part(0, 0) + near_top + chain_top
    bottom = part(0, 1) + near_bottom + chain_bottom
    return jnp.concatenate([top, bottom])


def on_device(
    feature_codes,
    bit_widths,
    row_scales,
    weight,
    layer_bias,
    adjacency_blocks,
    block_index,
    block_counts,
):
    row, col = lax.axis_index("row"), lax.axis_index("col")
    shift = 8 - bit_widths[0]
    level = jnp.left_shift(jnp.right_shift(feature_codes, shift), shift)
    features = (level.astype(jnp.float32) * row_scales[:, None]).astype(jnp.bfloat16)
    pieces = gather_rows(features)
    weight_rows = gather_weight(weight)

    y, x, z = row // (NX * NZ), (row // NZ) % NX, row % NZ
    source, k = block_index[:, 0] // KPER, block_index[:, 0] % KPER
    dx = jnp.remainder(x - (source // NZ) % NX, NX)
    dy = jnp.remainder(y - source // (NX * NZ), NY)
    dz = jnp.remainder(z - source % NZ, NZ)
    live = jnp.arange(MAXB)[None, :] < block_counts
    index = jnp.where(live, ((dx * NY + dy) * NZ + dz) * KPER + k, SHARDS * KPER).reshape(RB * MAXB)

    chip, core = col // 2, col % 2
    step = jnp.arange(RB)
    d, other = (step // KPER) % NH, jnp.where(step < RB // 2, 1 - core, core)
    order = (jnp.remainder(chip + d, NH) * 2 + other) * KPER + step % KPER
    n = jnp.arange(NH * 2)
    place = jnp.remainder(chip - n // 2, NH) * 2 + (core ^ (n % 2))
    send, keep = aggregate(
        order.astype(jnp.int32), index.astype(jnp.int32), place.astype(jnp.int32), weight_rows, adjacency_blocks, pieces
    )
    summed = reduce_chips(send, keep)
    return jnp.maximum(summed + layer_bias[None, :], 0.0).astype(jnp.bfloat16)


def solution(mesh):
    in_specs = (
        P(("row", "col"), None),
        P(("row", "col")),
        P(("row", "col")),
        P("col", None),
        P(),
        P("row", "col", None, None, None),
        P("row", "col", None),
        P("row", "col"),
    )
    out_specs = P(("row", "col"), None)
    return jax.shard_map(
        on_device, mesh=mesh, in_specs=in_specs, out_specs=out_specs, check_vma=False
    )
```

```python
import functools

import jax
import jax.numpy as jnp
from jax import lax
from jax.experimental import pallas as pl
from jax.experimental.pallas import tpu as pltpu
from jax.sharding import PartitionSpec as P

NX, NY, NZ = 4, 4, 2
NH = 4
PANEL = 512
BLOCK = 128
F = 256
RB = 32
MAXB = 11
KPER = PANEL // BLOCK
SHARDS = NX * NY * NZ
ADJ_COPIES = 4
TILE = 6
KERNEL_VMEM = 24 << 20

PLAN = (
    (1, 1, ((0, 0, 0),)),
    (0, -1, ((0, 0, 0),)),
    (2, 1, ((0, 0, 0),)),
    (0, 1, ((0, 0, 0),)),
    (1, -1, ((0, 0, 0),)),
    (1, 1, ((0, 1, 0),)),
    (0, -1, ((3, 0, 0),)),
    (2, 1, ((3, 0, 0), (0, 1, 0))),
    (0, 1, ((0, 0, 1),)),
    (1, -1, ((3, 0, 0),)),
    (1, 1, ((3, 0, 0), (1, 0, 0))),
    (0, -1, ((0, 2, 0),)),
    (0, 1, ((1, 0, 1),)),
    (1, -1, ((1, 0, 1), (2, 0, 0), (1, 0, 0))),
    (2, 1, ((0, 2, 0),)),
    (0, -1, ((3, 2, 0),)),
    (0, 1, ((0, 2, 0), (0, 1, 1))),
    (1, 1, ((2, 0, 0), (3, 0, 1), (2, 0, 1))),
    (2, 1, ((0, 3, 0),)),
    (0, -1, ((0, 2, 1),)),
    (2, 1, ((3, 3, 0),)),
    (0, -1, ((3, 2, 1),)),
    (0, 1, ((0, 2, 1),)),
    (1, -1, ((2, 0, 1),)),
)
LATE = (17, 20, 21, 22, 23)
WEIGHT_AFTER = (5, 10)


def row_perm(axis, step):
    pairs = []
    for y in range(NY):
        for x in range(NX):
            for z in range(NZ):
                c = [x, y, z]
                c[axis] = (c[axis] + step) % (NX, NY, NZ)[axis]
                pairs.append(((y * NX + x) * NZ + z, (c[1] * NX + c[0]) * NZ + c[2]))
    return pairs


def col_perm(dz, core):
    return [(h * 2 + c, ((h + dz) % NH) * 2 + (c ^ core)) for h in range(NH) for c in range(2)]


def after(value, *others):
    return lax.optimization_barrier((value, *others))[0]


def moved(place, axis, step):
    place = list(place)
    place[axis] = (place[axis] + step) % (NX, NY, NZ)[axis]
    return tuple(place)


def gather_rows(mine):
    arrays, at, last = [(mine, ((0, 0, 0),))], {(0, 0, 0): (0, 0)}, {}
    for axis, step, sources in PLAN:
        index = at[sources[0]][0]
        if arrays[index][1] == sources:
            value = arrays[index][0]
        else:
            rows = []
            for source in sources:
                index, n = at[source]
                array = arrays[index][0]
                rows.append(array if len(arrays[index][1]) == 1 else array[n * PANEL : (n + 1) * PANEL])
            value = rows[0] if len(rows) == 1 else jnp.concatenate(rows)
        link = (axis, step)
        if link in last:
            value = after(value, last[link])
        last[link] = got = lax.ppermute(value, "row", row_perm(axis, step))
        places = tuple(moved(source, axis, step) for source in sources)
        for n, place in enumerate(places):
            at[place] = (len(arrays), n)
        arrays.append((got, places))
    return arrays


def gather_weight(weight, arrays):
    pair = jnp.concatenate([weight, lax.ppermute(weight, "col", col_perm(0, 1))])
    pair = after(pair, arrays[1 + WEIGHT_AFTER[0]][0])
    quad = jnp.concatenate([pair, lax.ppermute(pair, "col", col_perm(1, 0))])
    quad = after(quad, arrays[1 + WEIGHT_AFTER[1]][0])
    whole = jnp.concatenate([quad, lax.ppermute(quad, "col", col_perm(2, 0))])
    return whole.reshape(NH * 2, F // (NH * 2), F)


def lay_weight(here_ref, weight_ref, weight):
    col = here_ref[1]
    rows = F // (NH * 2)
    for n in range(NH * 2):
        place = ((lax.shift_right_logical(col, 1) - n // 2) & (NH - 1)) * 2 + ((col & 1) ^ (n % 2))
        weight[pl.ds(pl.multiple_of(place * rows, rows), rows), :] = weight_ref[n]


def copies_of(refs, places, target, sems):
    copies, at = [], 0
    for n, ref in enumerate(refs):
        rows = len(places[n]) * PANEL
        copies.append(pltpu.make_async_copy(ref, target.at[pl.ds(at, rows)], sems.at[n]))
        at += rows
    return copies


def early_kernel(places, here_ref, weight_ref, adj_hbm, *refs):
    pieces = refs[: len(places)]
    hidden, adj, weight, adj_sems, sems = refs[len(places) :]
    copies = copies_of(pieces, places, hidden, sems)
    part = RB // ADJ_COPIES
    adj_copies = [
        pltpu.make_async_copy(adj_hbm.at[pl.ds(n * part, part), 0], adj.at[pl.ds(n * part, part)], adj_sems.at[n])
        for n in range(ADJ_COPIES)
    ]
    for copy in copies:
        copy.start()
    for copy in adj_copies:
        copy.start()
    lay_weight(here_ref, weight_ref, weight)
    hidden[pl.ds(SHARDS * PANEL, BLOCK), :] = jnp.zeros((BLOCK, F), jnp.bfloat16)
    total, ready, done = sum(len(p) for p in places), 0, 0
    for n, copy in enumerate(copies):
        copy.wait()
        ready += len(places[n])
        if ready - done >= TILE or ready == total:
            at = pl.ds(done * PANEL, (ready - done) * PANEL)
            hidden[at, :] = jnp.dot(
                hidden[at, :], weight[...], preferred_element_type=jnp.float32
            ).astype(jnp.bfloat16)
            done = ready
    for copy in adj_copies:
        copy.wait()


def early(here, weight_rows, adjacency, pieces, places):
    smem, vmem, anywhere = (pl.BlockSpec(memory_space=m) for m in (pltpu.SMEM, pltpu.VMEM, pl.ANY))
    return pl.pallas_call(
        functools.partial(early_kernel, places),
        in_specs=[smem, vmem, anywhere] + [anywhere] * len(pieces),
        out_specs=[vmem, vmem],
        scratch_shapes=[
            pltpu.VMEM((F, F), jnp.bfloat16),
            pltpu.SemaphoreType.DMA((ADJ_COPIES,)),
            pltpu.SemaphoreType.DMA((len(pieces),)),
        ],
        out_shape=[
            pltpu.VMEM((SHARDS * PANEL + BLOCK, F), jnp.bfloat16),
            pltpu.VMEM((RB, MAXB, BLOCK, BLOCK), jnp.bfloat16),
        ],
        compiler_params=pltpu.CompilerParams(vmem_limit_bytes=KERNEL_VMEM),
        cost_estimate=pl.CostEstimate(flops=2 * 13000 * F * F, bytes_accessed=20 << 20, transcendentals=0),
    )(here, weight_rows, adjacency, *pieces)


def late_kernel(places, before, here_ref, index_ref, count_ref, weight_ref, hidden_in, adj_in, *refs):
    pieces = refs[: len(places)]
    send_ref, keep_ref, hidden, adj, weight, table = refs[len(places) :]
    del hidden_in, adj_in
    lay_weight(here_ref, weight_ref, weight)
    row, col = here_ref[0], here_ref[1]
    y, x, z = lax.shift_right_logical(row, 3), lax.shift_right_logical(row, 1) & (NX - 1), row & (NZ - 1)
    order = [place for group in before + places for place in group]
    for n, (dx, dy, dz) in enumerate(order):
        shard = (((y - dy) & (NY - 1)) * NX + ((x - dx) & (NX - 1))) * NZ + (z ^ dz)
        table[shard] = n * PANEL
    at = sum(len(p) for p in before) * PANEL
    for piece in pieces:
        rows = pl.ds(at, piece.shape[0])
        hidden[rows, :] = jnp.dot(piece[...], weight[...], preferred_element_type=jnp.float32).astype(jnp.bfloat16)
        at += piece.shape[0]
    chip, core = lax.shift_right_logical(col, 1), col & 1

    def rows_at(block, m):
        column = index_ref[block, 0, m]
        start = table[lax.shift_right_logical(column, 2)] + (column & (KPER - 1)) * BLOCK
        start = jnp.where(m < count_ref[block, 0], start, SHARDS * PANEL)
        return hidden[pl.ds(pl.multiple_of(start, BLOCK), BLOCK), :]

    def total_of(block):
        right = [rows_at(block, m) for m in range(MAXB)]
        left = [adj[block, m] for m in range(MAXB)]
        return jnp.dot(
            jnp.concatenate(left, axis=1), jnp.concatenate(right, axis=0), preferred_element_type=jnp.float32
        )

    def panels(side, out_ref):
        def body(d, _):
            panel = ((chip + d) & (NH - 1)) * 2 + side
            for j in range(KPER):
                at = pl.ds(pl.multiple_of(d * PANEL + j * BLOCK, BLOCK), BLOCK)
                out_ref[at, :] = total_of(panel * KPER + j).astype(out_ref.dtype)
            return 0

        lax.fori_loop(0, NH, body, 0)

    panels(core ^ 1, send_ref)
    panels(core, keep_ref)


def late(here, index, counts, weight_rows, hidden, adj, pieces, places, before):
    smem, vmem = (pl.BlockSpec(memory_space=m) for m in (pltpu.SMEM, pltpu.VMEM))
    return pl.pallas_call(
        functools.partial(late_kernel, places, before),
        in_specs=[smem, smem, smem, vmem, vmem, vmem] + [vmem] * len(pieces),
        out_specs=[vmem, vmem, vmem, vmem],
        scratch_shapes=[
            pltpu.VMEM((F, F), jnp.bfloat16),
            pltpu.SMEM((SHARDS,), jnp.int32),
        ],
        out_shape=[
            pltpu.VMEM((NH * PANEL, F), jnp.bfloat16),
            pltpu.VMEM((NH * PANEL, F), jnp.float32),
            pltpu.VMEM((SHARDS * PANEL + BLOCK, F), jnp.bfloat16),
            pltpu.VMEM((RB, MAXB, BLOCK, BLOCK), jnp.bfloat16),
        ],
        input_output_aliases={4: 2, 5: 3},
        compiler_params=pltpu.CompilerParams(vmem_limit_bytes=KERNEL_VMEM),
    )(here, index, counts, weight_rows, hidden, adj, *pieces)


def reduce_chips(send, keep):
    got = lax.ppermute(send, "col", col_perm(0, 1))
    h = PANEL // 2

    def part(d, side):
        at = d * PANEL + side * h
        return keep[at : at + h] + got[at : at + h].astype(jnp.float32)

    def plus(value):
        return lax.ppermute(value.astype(jnp.bfloat16), "col", col_perm(1, 0)).astype(jnp.float32)

    def minus(value):
        return lax.ppermute(value.astype(jnp.bfloat16), "col", col_perm(-1, 0)).astype(jnp.float32)

    first = [part(2, 0), part(2, 1), part(1, 1), part(3, 0)]
    first = lax.optimization_barrier([value.astype(jnp.bfloat16) for value in first])
    far_top, far_bottom = plus(first[0]), minus(first[1])
    near_bottom, near_top = plus(first[2]), minus(first[3])
    chain_top = plus(part(1, 0) + far_top)
    chain_bottom = minus(part(3, 1) + far_bottom)
    top = part(0, 0) + near_top + chain_top
    bottom = part(0, 1) + near_bottom + chain_bottom
    return jnp.concatenate([top, bottom])


def on_device(
    feature_codes,
    bit_widths,
    row_scales,
    weight,
    layer_bias,
    adjacency_blocks,
    block_index,
    block_counts,
):
    here = jnp.stack([lax.axis_index("row"), lax.axis_index("col")]).astype(jnp.int32)
    shift = 8 - bit_widths[0]
    level = jnp.left_shift(jnp.right_shift(feature_codes, shift), shift)
    features = (level.astype(jnp.float32) * row_scales[:, None]).astype(jnp.bfloat16)
    arrays = gather_rows(features)
    weight_rows = gather_weight(weight, arrays)

    soon = [a for n, a in enumerate(arrays) if n - 1 not in LATE]
    last = [arrays[n + 1] for n in LATE]
    soon_places, last_places = [p for _, p in soon], [p for _, p in last]
    hidden, adj = early(here, weight_rows, adjacency_blocks, [a for a, _ in soon], soon_places)
    send, keep, _, _ = late(
        here, block_index, block_counts, weight_rows, hidden, adj, [a for a, _ in last], last_places, soon_places
    )
    summed = reduce_chips(send, keep)
    return jnp.maximum(summed + layer_bias[None, :], 0.0).astype(jnp.bfloat16)


def solution(mesh):
    in_specs = (
        P(("row", "col"), None),
        P(("row", "col")),
        P(("row", "col")),
        P("col", None),
        P(),
        P("row", "col", None, None, None),
        P("row", "col", None),
        P("row", "col"),
    )
    out_specs = P(("row", "col"), None)
    return jax.shard_map(
        on_device, mesh=mesh, in_specs=in_specs, out_specs=out_specs, check_vma=False
    )
```

```python
import functools

import jax
import jax.numpy as jnp
from jax import lax
from jax.experimental import pallas as pl
from jax.experimental.pallas import tpu as pltpu
from jax.sharding import PartitionSpec as P

NX, NY, NZ = 4, 4, 2
NH = 4
PANEL = 512
BLOCK = 128
F = 256
RB = 32
MAXB = 11
KPER = PANEL // BLOCK
SHARDS = NX * NY * NZ
ADJ_COPIES = 4
KERNEL_VMEM = 20 << 20
HIDDEN = pltpu.VMEM((SHARDS * PANEL + BLOCK, F), jnp.bfloat16)
ADJ = pltpu.VMEM((RB, MAXB, BLOCK, BLOCK), jnp.bfloat16)

PLAN = (
    (0, -1, ((0, 0, 0),)),
    (1, 1, ((0, 0, 0),)),
    (1, -1, ((0, 0, 0),)),
    (0, 1, ((0, 0, 0),)),
    (0, -1, ((3, 0, 0),)),
    (1, 1, ((3, 0, 0),)),
    (1, -1, ((0, 3, 0),)),
    (0, 1, ((0, 3, 0),)),
    (2, 1, ((0, 1, 0),)),
    (0, -1, ((0, 3, 0),)),
    (1, 1, ((1, 0, 0),)),
    (1, -1, ((2, 0, 0),)),
    (0, 1, ((0, 2, 0),)),
    (2, 1, ((0, 3, 0),)),
    (0, -1, ((0, 2, 0),)),
    (1, 1, ((2, 0, 0),)),
    (1, -1, ((2, 3, 0),)),
    (0, 1, ((0, 1, 1),)),
    (2, 1, ((2, 3, 0),)),
    (0, -1, ((0, 1, 1),)),
    (1, 1, ((0, 1, 1),)),
    (1, -1, ((0, 1, 1),)),
    (0, 1, ((0, 3, 1),)),
    (2, 1, ((1, 0, 0),)),
    (0, -1, ((3, 1, 1),)),
    (1, 1, ((2, 3, 1),)),
    (0, 1, ((0, 2, 1),)),
    (2, 1, ((3, 3, 0),)),
    (1, -1, ((3, 1, 1),)),
    (0, -1, ((0, 2, 1),)),
    (1, 1, ((2, 1, 1),)),
)
LATE = (26, 27, 28, 29, 30)


def row_perm(axis, step):
    pairs = []
    for y in range(NY):
        for x in range(NX):
            for z in range(NZ):
                c = [x, y, z]
                c[axis] = (c[axis] + step) % (NX, NY, NZ)[axis]
                pairs.append(((y * NX + x) * NZ + z, (c[1] * NX + c[0]) * NZ + c[2]))
    return pairs


def col_perm(dz, core):
    return [(h * 2 + c, ((h + dz) % NH) * 2 + (c ^ core)) for h in range(NH) for c in range(2)]


def after(value, *others):
    return lax.optimization_barrier((value, *others))[0]


def moved(place, axis, step):
    place = list(place)
    place[axis] = (place[axis] + step) % (NX, NY, NZ)[axis]
    return tuple(place)


def gather_rows(mine, before_z):
    arrays, at, last = [(mine, ((0, 0, 0),))], {(0, 0, 0): (0, 0)}, {}
    for axis, step, sources in PLAN:
        index = at[sources[0]][0]
        if arrays[index][1] == sources:
            value = arrays[index][0]
        else:
            rows = []
            for source in sources:
                index, n = at[source]
                array = arrays[index][0]
                rows.append(array if len(arrays[index][1]) == 1 else array[n * PANEL : (n + 1) * PANEL])
            value = rows[0] if len(rows) == 1 else jnp.concatenate(rows)
        link = (axis, step)
        if link in last:
            value = after(value, last[link])
        elif axis == 2:
            value = after(value, before_z)
        last[link] = got = lax.ppermute(value, "row", row_perm(axis, step))
        places = tuple(moved(source, axis, step) for source in sources)
        for n, place in enumerate(places):
            at[place] = (len(arrays), n)
        arrays.append((got, places))
    return arrays


def gather_weight(weight):
    pair = jnp.concatenate([weight, lax.ppermute(weight, "col", col_perm(0, 1))])
    quad = jnp.concatenate([pair, lax.ppermute(pair, "col", col_perm(1, 0))])
    whole = jnp.concatenate([quad, lax.ppermute(quad, "col", col_perm(2, 0))])
    return whole.reshape(NH * 2, F // (NH * 2), F)


def lay_weight(here_ref, weight_ref, weight):
    col = here_ref[1]
    rows = F // (NH * 2)
    for n in range(NH * 2):
        place = ((lax.shift_right_logical(col, 1) - n // 2) & (NH - 1)) * 2 + ((col & 1) ^ (n % 2))
        weight[pl.ds(pl.multiple_of(place * rows, rows), rows), :] = weight_ref[n]


def hidden_rows(pieces, weight, hidden, at):
    for piece in pieces:
        rows = pl.ds(at, piece.shape[0])
        hidden[rows, :] = jnp.dot(piece[...], weight[...], preferred_element_type=jnp.float32).astype(jnp.bfloat16)
        at += piece.shape[0]


def early_kernel(here_ref, weight_ref, adj_hbm, *refs):
    *pieces, hidden, adj, weight, sems = refs
    part = RB // ADJ_COPIES
    copies = [
        pltpu.make_async_copy(adj_hbm.at[pl.ds(n * part, part), 0], adj.at[pl.ds(n * part, part)], sems.at[n])
        for n in range(ADJ_COPIES)
    ]
    for copy in copies:
        copy.start()
    lay_weight(here_ref, weight_ref, weight)
    hidden[pl.ds(SHARDS * PANEL, BLOCK), :] = jnp.zeros((BLOCK, F), jnp.bfloat16)
    hidden_rows(pieces, weight, hidden, 0)
    for copy in copies:
        copy.wait()


def early(here, weight_rows, adjacency, pieces):
    smem, vmem, anywhere = (pl.BlockSpec(memory_space=m) for m in (pltpu.SMEM, pltpu.VMEM, pl.ANY))
    return pl.pallas_call(
        early_kernel,
        in_specs=[smem, vmem, anywhere] + [vmem] * len(pieces),
        out_specs=[vmem, vmem],
        scratch_shapes=[pltpu.VMEM((F, F), jnp.bfloat16), pltpu.SemaphoreType.DMA((ADJ_COPIES,))],
        out_shape=[HIDDEN, ADJ],
        compiler_params=pltpu.CompilerParams(vmem_limit_bytes=KERNEL_VMEM),
        cost_estimate=pl.CostEstimate(flops=2 * 13000 * F * F, bytes_accessed=20 << 20, transcendentals=0),
    )(here, weight_rows, adjacency, *pieces)


def products(here_ref, index_ref, count_ref, hidden, adj, table, order, side, out_ref):
    row, col = here_ref[0], here_ref[1]
    y, x, z = lax.shift_right_logical(row, 3), lax.shift_right_logical(row, 1) & (NX - 1), row & (NZ - 1)
    chip, core = lax.shift_right_logical(col, 1), (col & 1) ^ side
    for n, (dx, dy, dz) in enumerate(order):
        shard = (((y - dy) & (NY - 1)) * NX + ((x - dx) & (NX - 1))) * NZ + (z ^ dz)
        table[shard] = n * PANEL

    def rows_at(block, m):
        column = index_ref[block, 0, m]
        start = table[lax.shift_right_logical(column, 2)] + (column & (KPER - 1)) * BLOCK
        start = jnp.where(m < count_ref[block, 0], start, SHARDS * PANEL)
        return hidden[pl.ds(pl.multiple_of(start, BLOCK), BLOCK), :]

    def total_of(block):
        right = [rows_at(block, m) for m in range(MAXB)]
        left = [adj[block, m] for m in range(MAXB)]
        return jnp.dot(
            jnp.concatenate(left, axis=1), jnp.concatenate(right, axis=0), preferred_element_type=jnp.float32
        )

    def body(d, _):
        panel = ((chip + d) & (NH - 1)) * 2 + core
        for j in range(KPER):
            at = pl.ds(pl.multiple_of(d * PANEL + j * BLOCK, BLOCK), BLOCK)
            out_ref[at, :] = total_of(panel * KPER + j).astype(out_ref.dtype)
        return 0

    lax.fori_loop(0, NH, body, 0)


def send_kernel(order, here_ref, index_ref, count_ref, hidden_in, adj_in, weight_ref, *refs):
    *pieces, send_ref, hidden, adj, weight, table = refs
    del hidden_in, adj_in
    lay_weight(here_ref, weight_ref, weight)
    hidden_rows(pieces, weight, hidden, SHARDS * PANEL - sum(piece.shape[0] for piece in pieces))
    products(here_ref, index_ref, count_ref, hidden, adj, table, order, 1, send_ref)


def keep_kernel(order, here_ref, index_ref, count_ref, hidden_in, adj_in, keep_ref, hidden, adj, table):
    del hidden_in, adj_in
    products(here_ref, index_ref, count_ref, hidden, adj, table, order, 0, keep_ref)


def aggregate(kernel, order, dtype, here, index, counts, hidden, adj, *more):
    smem, vmem = (pl.BlockSpec(memory_space=m) for m in (pltpu.SMEM, pltpu.VMEM))
    weight = [pltpu.VMEM((F, F), jnp.bfloat16)] if more else []
    return pl.pallas_call(
        functools.partial(kernel, order),
        in_specs=[smem, smem, smem, vmem, vmem] + [vmem] * len(more),
        out_specs=[vmem, vmem, vmem],
        scratch_shapes=weight + [pltpu.SMEM((SHARDS,), jnp.int32)],
        out_shape=[pltpu.VMEM((NH * PANEL, F), dtype), HIDDEN, ADJ],
        input_output_aliases={3: 1, 4: 2},
        compiler_params=pltpu.CompilerParams(vmem_limit_bytes=KERNEL_VMEM),
        cost_estimate=pl.CostEstimate(flops=1500000000, bytes_accessed=8 << 20, transcendentals=0),
    )(here, index, counts, hidden, adj, *more)


def reduce_chips(got, keep):
    h = PANEL // 2

    def part(d, side):
        at = d * PANEL + side * h
        return keep[at : at + h] + got[at : at + h].astype(jnp.float32)

    def plus(value):
        return lax.ppermute(value.astype(jnp.bfloat16), "col", col_perm(1, 0)).astype(jnp.float32)

    def minus(value):
        return lax.ppermute(value.astype(jnp.bfloat16), "col", col_perm(-1, 0)).astype(jnp.float32)

    first = [part(2, 0), part(2, 1), part(1, 1), part(3, 0)]
    first = lax.optimization_barrier([value.astype(jnp.bfloat16) for value in first])
    far_top, far_bottom = plus(first[0]), minus(first[1])
    near_bottom, near_top = plus(first[2]), minus(first[3])
    chain_top = plus(part(1, 0) + far_top)
    chain_bottom = minus(part(3, 1) + far_bottom)
    top = part(0, 0) + near_top + chain_top
    bottom = part(0, 1) + near_bottom + chain_bottom
    return jnp.concatenate([top, bottom])


def on_device(
    feature_codes,
    bit_widths,
    row_scales,
    weight,
    layer_bias,
    adjacency_blocks,
    block_index,
    block_counts,
):
    here = jnp.stack([lax.axis_index("row"), lax.axis_index("col")]).astype(jnp.int32)
    shift = 8 - bit_widths[0]
    level = jnp.left_shift(jnp.right_shift(feature_codes, shift), shift)
    features = (level.astype(jnp.float32) * row_scales[:, None]).astype(jnp.bfloat16)
    weight_rows = gather_weight(weight)
    arrays = gather_rows(features, weight_rows)

    soon = [a for n, a in enumerate(arrays) if n - 1 not in LATE]
    last = [arrays[n + 1] for n in LATE]
    order = [place for _, places in soon + last for place in places]
    blocks = pltpu.with_memory_space_constraint(adjacency_blocks, pltpu.HBM)
    hidden, adj = early(here, weight_rows, blocks, [a for a, _ in soon])
    tables = (here, block_index, block_counts)
    send, hidden, adj = aggregate(
        send_kernel, order, jnp.bfloat16, *tables, hidden, adj, weight_rows, *[a for a, _ in last]
    )
    got = lax.ppermute(send, "col", col_perm(0, 1))
    keep, _, _ = aggregate(keep_kernel, order, jnp.float32, *tables, hidden, adj)
    summed = reduce_chips(got, keep)
    return jnp.maximum(summed + layer_bias[None, :], 0.0).astype(jnp.bfloat16)


def solution(mesh):
    in_specs = (
        P(("row", "col"), None),
        P(("row", "col")),
        P(("row", "col")),
        P("col", None),
        P(),
        P("row", "col", None, None, None),
        P("row", "col", None),
        P("row", "col"),
    )
    out_specs = P(("row", "col"), None)
    return jax.shard_map(
        on_device, mesh=mesh, in_specs=in_specs, out_specs=out_specs, check_vma=False
    )
```

```python
import functools

import jax
import jax.numpy as jnp
from jax import lax
from jax.experimental import pallas as pl
from jax.experimental.pallas import tpu as pltpu
from jax.sharding import PartitionSpec as P

NX, NY, NZ = 4, 4, 2
NH = 4
PANEL = 512
BLOCK = 128
F = 256
RB = 32
MAXB = 11
KPER = PANEL // BLOCK
SHARDS = NX * NY * NZ
STOPS = (9, 18, 27)
KERNEL_VMEM = 16 << 20
EARLY_VMEM = 36 << 20
HIDDEN = pltpu.VMEM((SHARDS * PANEL + BLOCK, F), jnp.bfloat16)
ADJ = pltpu.VMEM((RB // 2, MAXB, BLOCK, BLOCK), jnp.bfloat16)

PLAN = (
    (0, -1, ((0, 0, 0),)),
    (0, 1, ((0, 0, 0),)),
    (1, -1, ((0, 0, 0),)),
    (1, 1, ((0, 0, 0),)),
    (2, 1, ((0, 0, 0),)),
    (0, -1, ((0, 1, 0),)),
    (0, 1, ((0, 3, 0),)),
    (1, -1, ((3, 0, 0),)),
    (1, 1, ((0, 0, 1),)),
    (2, 1, ((1, 0, 0),)),
    (0, 1, ((1, 0, 0),)),
    (1, -1, ((0, 0, 1),)),
    (1, 1, ((0, 1, 0),)),
    (2, 1, ((3, 0, 0),)),
    (0, -1, ((0, 1, 1),)),
    (0, 1, ((0, 1, 0),)),
    (1, -1, ((3, 3, 0),)),
    (1, 1, ((0, 1, 1),)),
    (2, 1, ((1, 3, 0),)),
    (0, -1, ((3, 1, 0),)),
    (0, 1, ((0, 2, 0),)),
    (1, -1, ((2, 0, 0),)),
    (1, 1, ((1, 0, 1),)),
    (2, 1, ((2, 0, 0),)),
    (0, -1, ((3, 1, 1),)),
    (0, 1, ((1, 3, 1),)),
    (1, -1, ((1, 3, 1),)),
    (1, 1, ((2, 1, 0),)),
    (2, 1, ((3, 3, 0),)),
    (0, -1, ((0, 2, 1),)),
    (1, 1, ((2, 1, 1),)),
)
LATE = (25, 26, 28, 29, 30)


def row_perm(axis, step):
    pairs = []
    for y in range(NY):
        for x in range(NX):
            for z in range(NZ):
                c = [x, y, z]
                c[axis] = (c[axis] + step) % (NX, NY, NZ)[axis]
                pairs.append(((y * NX + x) * NZ + z, (c[1] * NX + c[0]) * NZ + c[2]))
    return pairs


def col_perm(dz, core):
    return [(h * 2 + c, ((h + dz) % NH) * 2 + (c ^ core)) for h in range(NH) for c in range(2)]


def after(value, *others):
    return lax.optimization_barrier((value, *others))[0]


def moved(place, axis, step):
    place = list(place)
    place[axis] = (place[axis] + step) % (NX, NY, NZ)[axis]
    return tuple(place)


def gather_rows(mine):
    arrays, at, last = [(mine, ((0, 0, 0),))], {(0, 0, 0): (0, 0)}, {}
    for axis, step, sources in PLAN:
        index = at[sources[0]][0]
        if arrays[index][1] == sources:
            value = arrays[index][0]
        else:
            rows = []
            for source in sources:
                index, n = at[source]
                array = arrays[index][0]
                rows.append(array if len(arrays[index][1]) == 1 else array[n * PANEL : (n + 1) * PANEL])
            value = rows[0] if len(rows) == 1 else jnp.concatenate(rows)
        link = (axis, step)
        if link in last:
            value = after(value, last[link])
        last[link] = got = lax.ppermute(value, "row", row_perm(axis, step))
        places = tuple(moved(source, axis, step) for source in sources)
        for n, place in enumerate(places):
            at[place] = (len(arrays), n)
        arrays.append((got, places))
    return arrays


def gather_weight(weight):
    pair = jnp.concatenate([weight, lax.ppermute(weight, "col", col_perm(0, 1))])
    return [pair] + [lax.ppermute(pair, "col", col_perm(d, 0)) for d in range(1, NH)]


def hidden_rows(pieces, weight, hidden, at):
    for piece in pieces:
        rows = pl.ds(at, piece.shape[0])
        hidden[rows, :] = jnp.dot(piece[...], weight[...], preferred_element_type=jnp.float32).astype(jnp.bfloat16)
        at += piece.shape[0]


def adjacency_copies(col, side, adj_hbm, adj, sems):
    chip, core = lax.shift_right_logical(col, 1), (col & 1) ^ side
    copies = []
    for d in range(NH):
        panel = ((chip + d) & (NH - 1)) * 2 + core
        source = adj_hbm.at[pl.ds(panel * KPER, KPER), 0]
        copies.append(pltpu.make_async_copy(source, adj.at[pl.ds(d * KPER, KPER)], sems.at[d]))
    return copies


def early_kernel(here_ref, adj_hbm, *refs):
    pairs, (*pieces, hidden, adj, weight, sems, weight_sems, piece_sems) = refs[:NH], refs[NH:]
    piece_copies = [
        pltpu.make_async_copy(piece, hidden.at[pl.ds(n * PANEL, PANEL)], piece_sems.at[n])
        for n, piece in enumerate(pieces)
    ]
    rows = F // (NH * 2)
    col = here_ref[1]
    weight_copies = []
    for n in range(NH * 2):
        place = ((lax.shift_right_logical(col, 1) - n // 2) & (NH - 1)) * 2 + ((col & 1) ^ (n % 2))
        source = pairs[n // 2].at[pl.ds(n % 2 * rows, rows)]
        target = weight.at[pl.ds(pl.multiple_of(place * rows, rows), rows)]
        weight_copies.append(pltpu.make_async_copy(source, target, weight_sems.at[n]))
    copies = adjacency_copies(here_ref[1], 1, adj_hbm, adj, sems)
    for copy in weight_copies + piece_copies + copies:
        copy.start()
    hidden[pl.ds(SHARDS * PANEL, BLOCK), :] = jnp.zeros((BLOCK, F), jnp.bfloat16)
    for copy in weight_copies:
        copy.wait()
    for n, copy in enumerate(piece_copies):
        copy.wait()
        if n + 1 in STOPS:
            first = max([0] + [stop for stop in STOPS if stop <= n])
            rows = pl.ds(first * PANEL, (n + 1 - first) * PANEL)
            hidden[rows, :] = jnp.dot(hidden[rows, :], weight[...], preferred_element_type=jnp.float32).astype(
                jnp.bfloat16
            )
    for copy in copies:
        copy.wait()


def early(here, pairs, adjacency, pieces):
    smem, vmem, anywhere = (pl.BlockSpec(memory_space=m) for m in (pltpu.SMEM, pltpu.VMEM, pl.ANY))
    return pl.pallas_call(
        early_kernel,
        in_specs=[smem, anywhere] + [anywhere] * (len(pairs) + len(pieces)),
        out_specs=[vmem, vmem, vmem],
        scratch_shapes=[pltpu.SemaphoreType.DMA((n,)) for n in (NH, NH * 2, len(pieces))],
        out_shape=[HIDDEN, ADJ, pltpu.VMEM((F, F), jnp.bfloat16)],
        compiler_params=pltpu.CompilerParams(vmem_limit_bytes=EARLY_VMEM),
        cost_estimate=pl.CostEstimate(flops=2 * 13000 * F * F, bytes_accessed=20 << 20, transcendentals=0),
    )(here, adjacency, *pairs, *pieces)


def products(here_ref, index_ref, count_ref, hidden, adj, table, order, side, out_ref):
    row, col = here_ref[0], here_ref[1]
    y, x, z = lax.shift_right_logical(row, 3), lax.shift_right_logical(row, 1) & (NX - 1), row & (NZ - 1)
    chip, core = lax.shift_right_logical(col, 1), (col & 1) ^ side
    for n, (dx, dy, dz) in enumerate(order):
        shard = (((y - dy) & (NY - 1)) * NX + ((x - dx) & (NX - 1))) * NZ + (z ^ dz)
        table[shard] = n * PANEL

    def rows_at(block, m):
        column = index_ref[block, 0, m]
        start = table[lax.shift_right_logical(column, 2)] + (column & (KPER - 1)) * BLOCK
        start = jnp.where(m < count_ref[block, 0], start, SHARDS * PANEL)
        return hidden[pl.ds(pl.multiple_of(start, BLOCK), BLOCK), :]

    def total_of(block, at):
        right = [rows_at(block, m) for m in range(MAXB)]
        left = [adj[at, m] for m in range(MAXB)]
        return jnp.dot(
            jnp.concatenate(left, axis=1), jnp.concatenate(right, axis=0), preferred_element_type=jnp.float32
        )

    def body(d, _):
        panel = ((chip + d) & (NH - 1)) * 2 + core
        for j in range(KPER):
            at = pl.ds(pl.multiple_of(d * PANEL + j * BLOCK, BLOCK), BLOCK)
            out_ref[at, :] = total_of(panel * KPER + j, d * KPER + j).astype(out_ref.dtype)
        return 0

    lax.fori_loop(0, NH, body, 0)


def send_kernel(order, here_ref, index_ref, count_ref, hidden_in, adj, adj_hbm, weight, *refs):
    *pieces, send_ref, hidden, next_adj, table, sems = refs
    del hidden_in
    copies = adjacency_copies(here_ref[1], 0, adj_hbm, next_adj, sems)
    for copy in copies:
        copy.start()
    hidden_rows(pieces, weight, hidden, SHARDS * PANEL - sum(piece.shape[0] for piece in pieces))
    products(here_ref, index_ref, count_ref, hidden, adj, table, order, 1, send_ref)
    for copy in copies:
        copy.wait()


def keep_kernel(order, here_ref, index_ref, count_ref, hidden, adj, keep_ref, table):
    products(here_ref, index_ref, count_ref, hidden, adj, table, order, 0, keep_ref)


def send_products(order, here, index, counts, hidden, adj, adjacency, weight, pieces):
    smem, vmem, anywhere = (pl.BlockSpec(memory_space=m) for m in (pltpu.SMEM, pltpu.VMEM, pl.ANY))
    return pl.pallas_call(
        functools.partial(send_kernel, order),
        in_specs=[smem, smem, smem, vmem, vmem, anywhere, vmem] + [vmem] * len(pieces),
        out_specs=[vmem, vmem, vmem],
        scratch_shapes=[pltpu.SMEM((SHARDS,), jnp.int32), pltpu.SemaphoreType.DMA((NH,))],
        out_shape=[pltpu.VMEM((NH * PANEL, F), jnp.bfloat16), HIDDEN, ADJ],
        input_output_aliases={3: 1},
        compiler_params=pltpu.CompilerParams(vmem_limit_bytes=KERNEL_VMEM),
        cost_estimate=pl.CostEstimate(flops=1500000000, bytes_accessed=8 << 20, transcendentals=0),
    )(here, index, counts, hidden, adj, adjacency, weight, *pieces)


def keep_products(order, here, index, counts, hidden, adj):
    smem, vmem = (pl.BlockSpec(memory_space=m) for m in (pltpu.SMEM, pltpu.VMEM))
    return pl.pallas_call(
        functools.partial(keep_kernel, order),
        in_specs=[smem, smem, smem, vmem, vmem],
        out_specs=vmem,
        scratch_shapes=[pltpu.SMEM((SHARDS,), jnp.int32)],
        out_shape=pltpu.VMEM((NH * PANEL, F), jnp.float32),
        compiler_params=pltpu.CompilerParams(vmem_limit_bytes=KERNEL_VMEM),
        cost_estimate=pl.CostEstimate(flops=1500000000, bytes_accessed=8 << 20, transcendentals=0),
    )(here, index, counts, hidden, adj)


def reduce_chips(got, keep):
    h = PANEL // 2

    def part(d, side):
        at = d * PANEL + side * h
        return keep[at : at + h] + got[at : at + h].astype(jnp.float32)

    def plus(value):
        return lax.ppermute(value.astype(jnp.bfloat16), "col", col_perm(1, 0)).astype(jnp.float32)

    def minus(value):
        return lax.ppermute(value.astype(jnp.bfloat16), "col", col_perm(-1, 0)).astype(jnp.float32)

    first = [part(2, 0), part(2, 1), part(1, 1), part(3, 0)]
    first = lax.optimization_barrier([value.astype(jnp.bfloat16) for value in first])
    far_top, far_bottom = plus(first[0]), minus(first[1])
    near_bottom, near_top = plus(first[2]), minus(first[3])
    chain_top = plus(part(1, 0) + far_top)
    chain_bottom = minus(part(3, 1) + far_bottom)
    top = part(0, 0) + near_top + chain_top
    bottom = part(0, 1) + near_bottom + chain_bottom
    return jnp.concatenate([top, bottom])


def on_device(
    feature_codes,
    bit_widths,
    row_scales,
    weight,
    layer_bias,
    adjacency_blocks,
    block_index,
    block_counts,
):
    here = jnp.stack([lax.axis_index("row"), lax.axis_index("col")]).astype(jnp.int32)
    shift = 8 - bit_widths[0]
    level = jnp.left_shift(jnp.right_shift(feature_codes, shift), shift)
    features = (level.astype(jnp.float32) * row_scales[:, None]).astype(jnp.bfloat16)
    pairs = gather_weight(weight)
    arrays = gather_rows(features)

    soon = [a for n, a in enumerate(arrays) if n - 1 not in LATE]
    last = [arrays[n + 1] for n in LATE]
    order = [place for _, places in soon + last for place in places]
    blocks = pltpu.with_memory_space_constraint(adjacency_blocks, pltpu.HBM)
    pieces = [pltpu.with_memory_space_constraint(a, pltpu.HBM) for a, _ in soon]
    hidden, adj, full_weight = early(here, pairs, blocks, pieces)
    tables = (here, block_index, block_counts)
    send, hidden, adj = send_products(order, *tables, hidden, adj, blocks, full_weight, [a for a, _ in last])
    got = lax.ppermute(send, "col", col_perm(0, 1))
    keep = keep_products(order, *tables, hidden, adj)
    summed = reduce_chips(got, keep)
    return jnp.maximum(summed + layer_bias[None, :], 0.0).astype(jnp.bfloat16)


def solution(mesh):
    in_specs = (
        P(("row", "col"), None),
        P(("row", "col")),
        P(("row", "col")),
        P("col", None),
        P(),
        P("row", "col", None, None, None),
        P("row", "col", None),
        P("row", "col"),
    )
    out_specs = P(("row", "col"), None)
    return jax.shard_map(
        on_device, mesh=mesh, in_specs=in_specs, out_specs=out_specs, check_vma=False
    )
```

```python
import functools

import jax
import jax.numpy as jnp
from jax import lax
from jax.experimental import pallas as pl
from jax.experimental.pallas import tpu as pltpu
from jax.sharding import PartitionSpec as P

NX, NY, NZ = 4, 4, 2
NH = 4
PANEL = 512
BLOCK = 128
F = 256
RB = 32
MAXB = 11
KPER = PANEL // BLOCK
SHARDS = NX * NY * NZ
STOPS = (9, 18, 27)
KERNEL_VMEM = 16 << 20
EARLY_VMEM = 36 << 20
HIDDEN = pltpu.VMEM((SHARDS * PANEL + BLOCK, F), jnp.bfloat16)
ADJ = pltpu.VMEM((RB // 2, MAXB, BLOCK, BLOCK), jnp.bfloat16)

PLAN = (
    (0, -1, ((0, 0, 0),)),
    (0, 1, ((0, 0, 0),)),
    (1, -1, ((0, 0, 0),)),
    (1, 1, ((0, 0, 0),)),
    (2, 1, ((0, 0, 0),)),
    (0, -1, ((0, 1, 0),)),
    (0, 1, ((0, 3, 0),)),
    (1, -1, ((3, 0, 0),)),
    (1, 1, ((0, 0, 1),)),
    (2, 1, ((1, 0, 0),)),
    (0, 1, ((1, 0, 0),)),
    (1, -1, ((0, 0, 1),)),
    (1, 1, ((0, 1, 0),)),
    (2, 1, ((3, 0, 0),)),
    (0, -1, ((0, 1, 1),)),
    (0, 1, ((0, 1, 0),)),
    (1, -1, ((3, 3, 0),)),
    (1, 1, ((0, 1, 1),)),
    (2, 1, ((1, 3, 0),)),
    (0, -1, ((3, 1, 0),)),
    (0, 1, ((0, 2, 0),)),
    (1, -1, ((2, 0, 0),)),
    (1, 1, ((1, 0, 1),)),
    (2, 1, ((2, 0, 0),)),
    (0, -1, ((3, 1, 1),)),
    (0, 1, ((1, 3, 1),)),
    (1, -1, ((1, 3, 1),)),
    (1, 1, ((2, 1, 0),)),
    (2, 1, ((3, 3, 0),)),
    (0, -1, ((0, 2, 1),)),
    (1, 1, ((2, 1, 1),)),
)
LATE = (25, 26, 28, 29, 30)


def row_perm(axis, step):
    pairs = []
    for y in range(NY):
        for x in range(NX):
            for z in range(NZ):
                c = [x, y, z]
                c[axis] = (c[axis] + step) % (NX, NY, NZ)[axis]
                pairs.append(((y * NX + x) * NZ + z, (c[1] * NX + c[0]) * NZ + c[2]))
    return pairs


def col_perm(dz, core):
    return [(h * 2 + c, ((h + dz) % NH) * 2 + (c ^ core)) for h in range(NH) for c in range(2)]


def after(value, *others):
    return lax.optimization_barrier((value, *others))[0]


def moved(place, axis, step):
    place = list(place)
    place[axis] = (place[axis] + step) % (NX, NY, NZ)[axis]
    return tuple(place)


def gather_rows(mine):
    arrays, at, last = [(mine, ((0, 0, 0),))], {(0, 0, 0): (0, 0)}, {}
    for axis, step, sources in PLAN:
        index = at[sources[0]][0]
        if arrays[index][1] == sources:
            value = arrays[index][0]
        else:
            rows = []
            for source in sources:
                index, n = at[source]
                array = arrays[index][0]
                rows.append(array if len(arrays[index][1]) == 1 else array[n * PANEL : (n + 1) * PANEL])
            value = rows[0] if len(rows) == 1 else jnp.concatenate(rows)
        link = (axis, step)
        if link in last:
            value = after(value, last[link])
        last[link] = got = lax.ppermute(value, "row", row_perm(axis, step))
        places = tuple(moved(source, axis, step) for source in sources)
        for n, place in enumerate(places):
            at[place] = (len(arrays), n)
        arrays.append((got, places))
    return arrays


def gather_weight(weight):
    pair = jnp.concatenate([weight, lax.ppermute(weight, "col", col_perm(0, 1))])
    return [pair] + [lax.ppermute(pair, "col", col_perm(d, 0)) for d in range(1, NH)]


def hidden_rows(pieces, weight, hidden, at):
    for piece in pieces:
        rows = pl.ds(at, piece.shape[0])
        hidden[rows, :] = jnp.dot(piece[...], weight[...], preferred_element_type=jnp.float32).astype(jnp.bfloat16)
        at += piece.shape[0]


def adjacency_copies(col, side, adj_hbm, adj, sems):
    chip, core = lax.shift_right_logical(col, 1), (col & 1) ^ side
    copies = []
    for d in range(NH):
        panel = ((chip + d) & (NH - 1)) * 2 + core
        source = adj_hbm.at[pl.ds(panel * KPER, KPER), 0]
        copies.append(pltpu.make_async_copy(source, adj.at[pl.ds(d * KPER, KPER)], sems.at[d]))
    return copies


def early_kernel(here_ref, adj_hbm, *refs):
    pairs, (*pieces, hidden, adj, weight, sems, weight_sems, piece_sems) = refs[:NH], refs[NH:]
    piece_copies = [
        pltpu.make_async_copy(piece, hidden.at[pl.ds(n * PANEL, PANEL)], piece_sems.at[n])
        for n, piece in enumerate(pieces)
    ]
    rows = F // (NH * 2)
    col = here_ref[1]
    weight_copies = []
    for n in range(NH * 2):
        place = ((lax.shift_right_logical(col, 1) - n // 2) & (NH - 1)) * 2 + ((col & 1) ^ (n % 2))
        source = pairs[n // 2].at[pl.ds(n % 2 * rows, rows)]
        target = weight.at[pl.ds(pl.multiple_of(place * rows, rows), rows)]
        weight_copies.append(pltpu.make_async_copy(source, target, weight_sems.at[n]))
    copies = adjacency_copies(here_ref[1], 1, adj_hbm, adj, sems)
    for copy in weight_copies + piece_copies + copies:
        copy.start()
    hidden[pl.ds(SHARDS * PANEL, BLOCK), :] = jnp.zeros((BLOCK, F), jnp.bfloat16)
    for copy in weight_copies:
        copy.wait()
    for n, copy in enumerate(piece_copies):
        copy.wait()
        if n + 1 in STOPS:
            first = max([0] + [stop for stop in STOPS if stop <= n])
            rows = pl.ds(first * PANEL, (n + 1 - first) * PANEL)
            hidden[rows, :] = jnp.dot(hidden[rows, :], weight[...], preferred_element_type=jnp.float32).astype(
                jnp.bfloat16
            )
    for copy in copies:
        copy.wait()


def early(here, pairs, adjacency, pieces):
    smem, vmem, anywhere = (pl.BlockSpec(memory_space=m) for m in (pltpu.SMEM, pltpu.VMEM, pl.ANY))
    return pl.pallas_call(
        early_kernel,
        in_specs=[smem, anywhere] + [anywhere] * (len(pairs) + len(pieces)),
        out_specs=[vmem, vmem, vmem],
        scratch_shapes=[pltpu.SemaphoreType.DMA((n,)) for n in (NH, NH * 2, len(pieces))],
        out_shape=[HIDDEN, ADJ, pltpu.VMEM((F, F), jnp.bfloat16)],
        compiler_params=pltpu.CompilerParams(vmem_limit_bytes=EARLY_VMEM),
        cost_estimate=pl.CostEstimate(flops=2 * 13000 * F * F, bytes_accessed=20 << 20, transcendentals=0),
    )(here, adjacency, *pairs, *pieces)


def products(here_ref, index_ref, count_ref, hidden, adj, table, order, side, out_ref):
    row, col = here_ref[0], here_ref[1]
    y, x, z = lax.shift_right_logical(row, 3), lax.shift_right_logical(row, 1) & (NX - 1), row & (NZ - 1)
    chip, core = lax.shift_right_logical(col, 1), (col & 1) ^ side
    for n, (dx, dy, dz) in enumerate(order):
        shard = (((y - dy) & (NY - 1)) * NX + ((x - dx) & (NX - 1))) * NZ + (z ^ dz)
        table[shard] = n * PANEL

    def rows_at(block, m):
        column = index_ref[m, 0, block]
        start = table[lax.shift_right_logical(column, 2)] + (column & (KPER - 1)) * BLOCK
        start = jnp.where(m < count_ref[0, block], start, SHARDS * PANEL)
        return hidden[pl.ds(pl.multiple_of(start, BLOCK), BLOCK), :]

    def total_of(block, at):
        right = [rows_at(block, m) for m in range(MAXB)]
        left = [adj[at, m] for m in range(MAXB)]
        return jnp.dot(
            jnp.concatenate(left, axis=1), jnp.concatenate(right, axis=0), preferred_element_type=jnp.float32
        )

    def body(d, _):
        panel = ((chip + d) & (NH - 1)) * 2 + core
        for j in range(KPER):
            at = pl.ds(pl.multiple_of(d * PANEL + j * BLOCK, BLOCK), BLOCK)
            out_ref[at, :] = total_of(panel * KPER + j, d * KPER + j).astype(out_ref.dtype)
        return 0

    lax.fori_loop(0, NH, body, 0)


def send_kernel(order, here_ref, index_ref, count_ref, hidden_in, adj, adj_hbm, weight, *refs):
    *pieces, send_ref, hidden, next_adj, table, sems = refs
    del hidden_in
    copies = adjacency_copies(here_ref[1], 0, adj_hbm, next_adj, sems)
    for copy in copies:
        copy.start()
    hidden_rows(pieces, weight, hidden, SHARDS * PANEL - sum(piece.shape[0] for piece in pieces))
    products(here_ref, index_ref, count_ref, hidden, adj, table, order, 1, send_ref)
    for copy in copies:
        copy.wait()


def keep_kernel(order, here_ref, index_ref, count_ref, hidden, adj, keep_ref, table):
    products(here_ref, index_ref, count_ref, hidden, adj, table, order, 0, keep_ref)


def send_products(order, here, index, counts, hidden, adj, adjacency, weight, pieces):
    smem, vmem, anywhere = (pl.BlockSpec(memory_space=m) for m in (pltpu.SMEM, pltpu.VMEM, pl.ANY))
    return pl.pallas_call(
        functools.partial(send_kernel, order),
        in_specs=[smem, smem, smem, vmem, vmem, anywhere, vmem] + [vmem] * len(pieces),
        out_specs=[vmem, vmem, vmem],
        scratch_shapes=[pltpu.SMEM((SHARDS,), jnp.int32), pltpu.SemaphoreType.DMA((NH,))],
        out_shape=[pltpu.VMEM((NH * PANEL, F), jnp.bfloat16), HIDDEN, ADJ],
        input_output_aliases={3: 1},
        compiler_params=pltpu.CompilerParams(vmem_limit_bytes=KERNEL_VMEM),
        cost_estimate=pl.CostEstimate(flops=1500000000, bytes_accessed=8 << 20, transcendentals=0),
    )(here, index, counts, hidden, adj, adjacency, weight, *pieces)


def keep_products(order, here, index, counts, hidden, adj):
    smem, vmem = (pl.BlockSpec(memory_space=m) for m in (pltpu.SMEM, pltpu.VMEM))
    return pl.pallas_call(
        functools.partial(keep_kernel, order),
        in_specs=[smem, smem, smem, vmem, vmem],
        out_specs=vmem,
        scratch_shapes=[pltpu.SMEM((SHARDS,), jnp.int32)],
        out_shape=pltpu.VMEM((NH * PANEL, F), jnp.float32),
        compiler_params=pltpu.CompilerParams(vmem_limit_bytes=KERNEL_VMEM),
        cost_estimate=pl.CostEstimate(flops=1500000000, bytes_accessed=8 << 20, transcendentals=0),
    )(here, index, counts, hidden, adj)


def reduce_chips(got, keep):
    h = PANEL // 2

    def part(d, side):
        at = d * PANEL + side * h
        return keep[at : at + h] + got[at : at + h].astype(jnp.float32)

    def plus(value):
        return lax.ppermute(value.astype(jnp.bfloat16), "col", col_perm(1, 0)).astype(jnp.float32)

    def minus(value):
        return lax.ppermute(value.astype(jnp.bfloat16), "col", col_perm(-1, 0)).astype(jnp.float32)

    first = [part(2, 0), part(2, 1), part(1, 1), part(3, 0)]
    first = lax.optimization_barrier([value.astype(jnp.bfloat16) for value in first])
    far_top, far_bottom = plus(first[0]), minus(first[1])
    near_bottom, near_top = plus(first[2]), minus(first[3])
    chain_up = (part(1, 0) + far_top).astype(jnp.bfloat16)
    chain_down = (part(3, 1) + far_bottom).astype(jnp.bfloat16)
    chain_top, chain_bottom = plus(chain_up), minus(chain_down)
    got, keep = lax.optimization_barrier((got, keep, chain_up, chain_down))[:2]
    top = part(0, 0) + near_top + chain_top
    bottom = part(0, 1) + near_bottom + chain_bottom
    return jnp.concatenate([top, bottom])


def on_device(
    feature_codes,
    bit_widths,
    row_scales,
    weight,
    layer_bias,
    adjacency_blocks,
    block_index,
    block_counts,
):
    here = jnp.stack([lax.axis_index("row"), lax.axis_index("col")]).astype(jnp.int32)
    shift = 8 - bit_widths[0]
    level = jnp.left_shift(jnp.right_shift(feature_codes, shift), shift)
    features = (level.astype(jnp.float32) * row_scales[:, None]).astype(jnp.bfloat16)
    pairs = gather_weight(weight)
    arrays = gather_rows(features)

    soon = [a for n, a in enumerate(arrays) if n - 1 not in LATE]
    last = [arrays[n + 1] for n in LATE]
    order = [place for _, places in soon + last for place in places]
    blocks = pltpu.with_memory_space_constraint(adjacency_blocks, pltpu.HBM)
    pieces = [pltpu.with_memory_space_constraint(a, pltpu.HBM) for a, _ in soon]
    hidden, adj, full_weight = early(here, pairs, blocks, pieces)
    tables = (here, block_index.transpose(2, 1, 0), block_counts.transpose(1, 0))
    send, hidden, adj = send_products(order, *tables, hidden, adj, blocks, full_weight, [a for a, _ in last])
    got = lax.ppermute(send, "col", col_perm(0, 1))
    keep = keep_products(order, *tables, hidden, adj)
    summed = reduce_chips(got, keep)
    return jnp.maximum(summed + layer_bias[None, :], 0.0).astype(jnp.bfloat16)


def solution(mesh):
    in_specs = (
        P(("row", "col"), None),
        P(("row", "col")),
        P(("row", "col")),
        P("col", None),
        P(),
        P("row", "col", None, None, None),
        P("row", "col", None),
        P("row", "col"),
    )
    out_specs = P(("row", "col"), None)
    return jax.shard_map(
        on_device, mesh=mesh, in_specs=in_specs, out_specs=out_specs, check_vma=False
    )
```

```python
import functools

import jax
import jax.numpy as jnp
from jax import lax
from jax.experimental import pallas as pl
from jax.experimental.pallas import tpu as pltpu
from jax.sharding import PartitionSpec as P

NX, NY, NZ = 4, 4, 2
NH = 4
PANEL = 512
BLOCK = 128
F = 256
RB = 32
MAXB = 11
KPER = PANEL // BLOCK
SHARDS = NX * NY * NZ
STOPS = (9, 18, 27)
KERNEL_VMEM = 16 << 20
EARLY_VMEM = 36 << 20
HIDDEN = pltpu.VMEM((SHARDS * PANEL + BLOCK, F), jnp.bfloat16)
SEND = ((1, 1), (2, 1), (3, 1))
KEEP = ((1, 0), (2, 0), (3, 0))
OWN = ((0, 1), (0, 0))


def adjacency_of(panels):
    return pltpu.VMEM((len(panels) * KPER, MAXB, BLOCK, BLOCK), jnp.bfloat16)


PLAN = (
    (0, -1, ((0, 0, 0),)),
    (0, 1, ((0, 0, 0),)),
    (1, -1, ((0, 0, 0),)),
    (1, 1, ((0, 0, 0),)),
    (2, 1, ((0, 0, 0),)),
    (0, -1, ((0, 1, 0),)),
    (0, 1, ((0, 3, 0),)),
    (1, -1, ((3, 0, 0),)),
    (1, 1, ((0, 0, 1),)),
    (2, 1, ((1, 0, 0),)),
    (0, 1, ((1, 0, 0),)),
    (1, -1, ((0, 0, 1),)),
    (1, 1, ((0, 1, 0),)),
    (2, 1, ((3, 0, 0),)),
    (0, -1, ((0, 1, 1),)),
    (0, 1, ((0, 1, 0),)),
    (1, -1, ((3, 3, 0),)),
    (1, 1, ((0, 1, 1),)),
    (2, 1, ((1, 3, 0),)),
    (0, -1, ((3, 1, 0),)),
    (0, 1, ((0, 2, 0),)),
    (1, -1, ((2, 0, 0),)),
    (1, 1, ((1, 0, 1),)),
    (2, 1, ((2, 0, 0),)),
    (0, -1, ((3, 1, 1),)),
    (0, 1, ((1, 3, 1),)),
    (1, -1, ((1, 3, 1),)),
    (1, 1, ((2, 1, 0),)),
    (2, 1, ((3, 3, 0),)),
    (0, -1, ((0, 2, 1),)),
    (1, 1, ((2, 1, 1),)),
)
LATE = (25, 26, 28, 29, 30)


def row_perm(axis, step):
    pairs = []
    for y in range(NY):
        for x in range(NX):
            for z in range(NZ):
                c = [x, y, z]
                c[axis] = (c[axis] + step) % (NX, NY, NZ)[axis]
                pairs.append(((y * NX + x) * NZ + z, (c[1] * NX + c[0]) * NZ + c[2]))
    return pairs


def col_perm(dz, core):
    return [(h * 2 + c, ((h + dz) % NH) * 2 + (c ^ core)) for h in range(NH) for c in range(2)]


def after(value, *others):
    return lax.optimization_barrier((value, *others))[0]


def moved(place, axis, step):
    place = list(place)
    place[axis] = (place[axis] + step) % (NX, NY, NZ)[axis]
    return tuple(place)


def gather_rows(mine):
    arrays, at, last = [(mine, ((0, 0, 0),))], {(0, 0, 0): (0, 0)}, {}
    for axis, step, sources in PLAN:
        index = at[sources[0]][0]
        if arrays[index][1] == sources:
            value = arrays[index][0]
        else:
            rows = []
            for source in sources:
                index, n = at[source]
                array = arrays[index][0]
                rows.append(array if len(arrays[index][1]) == 1 else array[n * PANEL : (n + 1) * PANEL])
            value = rows[0] if len(rows) == 1 else jnp.concatenate(rows)
        link = (axis, step)
        if link in last:
            value = after(value, last[link])
        last[link] = got = lax.ppermute(value, "row", row_perm(axis, step))
        places = tuple(moved(source, axis, step) for source in sources)
        for n, place in enumerate(places):
            at[place] = (len(arrays), n)
        arrays.append((got, places))
    return arrays


def gather_weight(weight):
    pair = jnp.concatenate([weight, lax.ppermute(weight, "col", col_perm(0, 1))])
    return [pair] + [lax.ppermute(pair, "col", col_perm(d, 0)) for d in range(1, NH)]


def hidden_rows(pieces, weight, hidden, at):
    for piece in pieces:
        rows = pl.ds(at, piece.shape[0])
        hidden[rows, :] = jnp.dot(piece[...], weight[...], preferred_element_type=jnp.float32).astype(jnp.bfloat16)
        at += piece.shape[0]


def panel_of(col, d, side):
    return ((lax.shift_right_logical(col, 1) + d) & (NH - 1)) * 2 + ((col & 1) ^ side)


def adjacency_copies(col, panels, adj_hbm, adj, sems):
    copies = []
    for n, (d, side) in enumerate(panels):
        source = adj_hbm.at[pl.ds(panel_of(col, d, side) * KPER, KPER), 0]
        copies.append(pltpu.make_async_copy(source, adj.at[pl.ds(n * KPER, KPER)], sems.at[n]))
    return copies


def early_kernel(here_ref, adj_hbm, *refs):
    pairs, (*pieces, hidden, adj, weight, sems, weight_sems, piece_sems) = refs[:NH], refs[NH:]
    piece_copies = [
        pltpu.make_async_copy(piece, hidden.at[pl.ds(n * PANEL, PANEL)], piece_sems.at[n])
        for n, piece in enumerate(pieces)
    ]
    rows = F // (NH * 2)
    col = here_ref[1]
    weight_copies = []
    for n in range(NH * 2):
        place = ((lax.shift_right_logical(col, 1) - n // 2) & (NH - 1)) * 2 + ((col & 1) ^ (n % 2))
        source = pairs[n // 2].at[pl.ds(n % 2 * rows, rows)]
        target = weight.at[pl.ds(pl.multiple_of(place * rows, rows), rows)]
        weight_copies.append(pltpu.make_async_copy(source, target, weight_sems.at[n]))
    copies = adjacency_copies(here_ref[1], SEND, adj_hbm, adj, sems)
    for copy in weight_copies + piece_copies + copies:
        copy.start()
    hidden[pl.ds(SHARDS * PANEL, BLOCK), :] = jnp.zeros((BLOCK, F), jnp.bfloat16)
    for copy in weight_copies:
        copy.wait()
    for n, copy in enumerate(piece_copies):
        copy.wait()
        if n + 1 in STOPS:
            first = max([0] + [stop for stop in STOPS if stop <= n])
            rows = pl.ds(first * PANEL, (n + 1 - first) * PANEL)
            hidden[rows, :] = jnp.dot(hidden[rows, :], weight[...], preferred_element_type=jnp.float32).astype(
                jnp.bfloat16
            )
    for copy in copies:
        copy.wait()


def early(here, pairs, adjacency, pieces):
    smem, vmem, anywhere = (pl.BlockSpec(memory_space=m) for m in (pltpu.SMEM, pltpu.VMEM, pl.ANY))
    return pl.pallas_call(
        early_kernel,
        in_specs=[smem, anywhere] + [anywhere] * (len(pairs) + len(pieces)),
        out_specs=[vmem, vmem, vmem],
        scratch_shapes=[pltpu.SemaphoreType.DMA((n,)) for n in (len(SEND), NH * 2, len(pieces))],
        out_shape=[HIDDEN, adjacency_of(SEND), pltpu.VMEM((F, F), jnp.bfloat16)],
        compiler_params=pltpu.CompilerParams(vmem_limit_bytes=EARLY_VMEM),
        cost_estimate=pl.CostEstimate(flops=2 * 13000 * F * F, bytes_accessed=20 << 20, transcendentals=0),
    )(here, adjacency, *pairs, *pieces)


def products(here_ref, index_ref, count_ref, hidden, adj, table, order, panels, out_refs):
    row = here_ref[0]
    y, x, z = lax.shift_right_logical(row, 3), lax.shift_right_logical(row, 1) & (NX - 1), row & (NZ - 1)
    for n, (dx, dy, dz) in enumerate(order):
        shard = (((y - dy) & (NY - 1)) * NX + ((x - dx) & (NX - 1))) * NZ + (z ^ dz)
        table[shard] = n * PANEL

    def rows_at(block, m):
        column = index_ref[m, 0, block]
        start = table[lax.shift_right_logical(column, 2)] + (column & (KPER - 1)) * BLOCK
        start = jnp.where(m < count_ref[0, block], start, SHARDS * PANEL)
        return hidden[pl.ds(pl.multiple_of(start, BLOCK), BLOCK), :]

    def panel_sums(n, d, side, out_ref, at):
        panel = panel_of(here_ref[1], d, side)
        for j in range(KPER):
            right = [rows_at(panel * KPER + j, m) for m in range(MAXB)]
            left = [adj[n * KPER + j, m] for m in range(MAXB)]
            total = jnp.dot(
                jnp.concatenate(left, axis=1), jnp.concatenate(right, axis=0), preferred_element_type=jnp.float32
            )
            rows = pl.ds(pl.multiple_of(at + j * BLOCK, BLOCK), BLOCK)
            out_ref[rows, :] = total.astype(out_ref.dtype)

    if len(out_refs) > 1:
        for n, (d, side) in enumerate(panels):
            panel_sums(n, d, side, out_refs[n], 0)
        return

    def body(n, _):
        panel_sums(n, panels[0][0] + n, panels[0][1], out_refs[0], n * PANEL)
        return 0

    lax.fori_loop(0, len(panels), body, 0)


def send_kernel(order, here_ref, index_ref, count_ref, hidden_in, adj, adj_hbm, weight, *refs):
    *pieces, send_ref, hidden, next_adj, table, sems = refs
    del hidden_in
    copies = adjacency_copies(here_ref[1], KEEP, adj_hbm, next_adj, sems)
    for copy in copies:
        copy.start()
    hidden_rows(pieces, weight, hidden, SHARDS * PANEL - sum(piece.shape[0] for piece in pieces))
    products(here_ref, index_ref, count_ref, hidden, adj, table, order, SEND, [send_ref])
    for copy in copies:
        copy.wait()


def keep_kernel(order, here_ref, index_ref, count_ref, hidden, adj, adj_hbm, keep_ref, next_adj, table, sems):
    copies = adjacency_copies(here_ref[1], OWN, adj_hbm, next_adj, sems)
    for copy in copies:
        copy.start()
    products(here_ref, index_ref, count_ref, hidden, adj, table, order, KEEP, [keep_ref])
    for copy in copies:
        copy.wait()


def own_kernel(order, here_ref, index_ref, count_ref, hidden, adj, send_ref, keep_ref, table):
    products(here_ref, index_ref, count_ref, hidden, adj, table, order, OWN, [send_ref, keep_ref])


def call(kernel, in_specs, out_shape, aliases, blocks, copies):
    sems = [pltpu.SemaphoreType.DMA((copies,))] if copies else []
    return pl.pallas_call(
        kernel,
        in_specs=[pl.BlockSpec(memory_space=m) for m in in_specs],
        out_specs=[pl.BlockSpec(memory_space=pltpu.VMEM)] * len(out_shape),
        scratch_shapes=[pltpu.SMEM((SHARDS,), jnp.int32)] + sems,
        out_shape=out_shape,
        input_output_aliases=aliases,
        compiler_params=pltpu.CompilerParams(vmem_limit_bytes=KERNEL_VMEM),
        cost_estimate=pl.CostEstimate(
            flops=blocks * MAXB * 2 * BLOCK * BLOCK * F, bytes_accessed=blocks << 18, transcendentals=0
        ),
    )


def send_products(order, tables, hidden, adj, adjacency, weight, pieces):
    smem, vmem = pltpu.SMEM, pltpu.VMEM
    out_shape = [vmem((len(SEND) * PANEL, F), jnp.bfloat16), HIDDEN, adjacency_of(KEEP)]
    in_specs = [smem] * 3 + [vmem, vmem, pl.ANY, vmem] + [vmem] * len(pieces)
    kernel = functools.partial(send_kernel, order)
    return call(kernel, in_specs, out_shape, {3: 1}, 12, len(KEEP))(*tables, hidden, adj, adjacency, weight, *pieces)


def keep_products(order, tables, hidden, adj, adjacency):
    smem, vmem = pltpu.SMEM, pltpu.VMEM
    out_shape = [vmem((len(KEEP) * PANEL, F), jnp.float32), adjacency_of(OWN)]
    kernel = functools.partial(keep_kernel, order)
    return call(kernel, [smem] * 3 + [vmem, vmem, pl.ANY], out_shape, {}, 12, len(OWN))(
        *tables, hidden, adj, adjacency
    )


def own_products(order, tables, hidden, adj):
    smem, vmem = pltpu.SMEM, pltpu.VMEM
    out_shape = [vmem((PANEL, F), jnp.bfloat16), vmem((PANEL, F), jnp.float32)]
    kernel = functools.partial(own_kernel, order)
    return call(kernel, [smem] * 3 + [vmem, vmem], out_shape, {}, 8, 0)(*tables, hidden, adj)


def reduce_chips(got, keep, own):
    h = PANEL // 2

    def part(d, side):
        at = (d - 1) * PANEL + side * h
        return keep[at : at + h] + got[at : at + h].astype(jnp.float32)

    def plus(value):
        return lax.ppermute(value.astype(jnp.bfloat16), "col", col_perm(1, 0)).astype(jnp.float32)

    def minus(value):
        return lax.ppermute(value.astype(jnp.bfloat16), "col", col_perm(-1, 0)).astype(jnp.float32)

    first = [part(2, 0), part(2, 1), part(1, 1), part(3, 0)]
    first = lax.optimization_barrier([value.astype(jnp.bfloat16) for value in first])
    far_top, far_bottom = plus(first[0]), minus(first[1])
    near_bottom, near_top = plus(first[2]), minus(first[3])
    chain_up = (part(1, 0) + far_top).astype(jnp.bfloat16)
    chain_down = (part(3, 1) + far_bottom).astype(jnp.bfloat16)
    chain_top, chain_bottom = plus(chain_up), minus(chain_down)
    got, keep = own(first[0], first[1])
    summed = keep + got.astype(jnp.float32)
    top = summed[:h] + near_top + chain_top
    bottom = summed[h:] + near_bottom + chain_bottom
    return jnp.concatenate([top, bottom])


def on_device(
    feature_codes,
    bit_widths,
    row_scales,
    weight,
    layer_bias,
    adjacency_blocks,
    block_index,
    block_counts,
):
    here = jnp.stack([lax.axis_index("row"), lax.axis_index("col")]).astype(jnp.int32)
    shift = 8 - bit_widths[0]
    level = jnp.left_shift(jnp.right_shift(feature_codes, shift), shift)
    features = (level.astype(jnp.float32) * row_scales[:, None]).astype(jnp.bfloat16)
    pairs = gather_weight(weight)
    arrays = gather_rows(features)

    soon = [a for n, a in enumerate(arrays) if n - 1 not in LATE]
    last = [arrays[n + 1] for n in LATE]
    order = [place for _, places in soon + last for place in places]
    blocks = pltpu.with_memory_space_constraint(adjacency_blocks, pltpu.HBM)
    pieces = [pltpu.with_memory_space_constraint(a, pltpu.HBM) for a, _ in soon]
    hidden, adj, full_weight = early(here, pairs, blocks, pieces)
    tables = (here, block_index.transpose(2, 1, 0), block_counts.transpose(1, 0))
    send, hidden, adj = send_products(order, tables, hidden, adj, blocks, full_weight, [a for a, _ in last])
    got = lax.ppermute(send, "col", col_perm(0, 1))
    keep, adj = keep_products(order, tables, hidden, adj, blocks)

    def own(*sums):
        own_send, own_keep = own_products(order, tables, hidden, after(adj, *sums))
        return lax.ppermute(own_send, "col", col_perm(0, 1)), own_keep

    summed = reduce_chips(got, keep, own)
    return jnp.maximum(summed + layer_bias[None, :], 0.0).astype(jnp.bfloat16)


def solution(mesh):
    in_specs = (
        P(("row", "col"), None),
        P(("row", "col")),
        P(("row", "col")),
        P("col", None),
        P(),
        P("row", "col", None, None, None),
        P("row", "col", None),
        P("row", "col"),
    )
    out_specs = P(("row", "col"), None)
    return jax.shard_map(
        on_device, mesh=mesh, in_specs=in_specs, out_specs=out_specs, check_vma=False
    )
```
